32 devices in a mesh: seq: 16 (over z, y, core), head: 2 (over x).
Axes of the slice: x: 2, y: 2, z: 4, core: 2. Of those that a mesh axis runs over, the one named last changes fastest.
Arguments:
- xin: bfloat16 [8192, 8192], P('seq', 'head'), may hold values from -6 to 6
- gate_z: bfloat16 [8192, 8192], P('seq', 'head'), may hold values from -6 to 6
- b_proj: bfloat16 [8192, 8, 256], P('seq', 'head'), may hold values from -0.375 to 0.375
- c_proj: bfloat16 [8192, 8, 256], P('seq', 'head'), may hold values from -0.375 to 0.375
- log_retain: float32 [8192, 128], P('seq', 'head'), may hold values from -2 to 0, as said below
- skip_d: float32 [128], P('head'), may hold values from 0.5 to 2
- norm_gain: float32 [8192], P('head'), may hold values from 0.5 to 1.5
- w_out: bfloat16 [8192, 4096], P('head', 'seq'), may hold values from -0.0625 to 0.0625
- residual: bfloat16 [8192, 4096], P(('seq', 'head')), may hold values from -24 to 24
- refusal: float32 [4096], replicated, may hold values from -6 to 6
- stream_gain: float32 [4096], replicated, may hold values from 0.5 to 1.5
- w_in: bfloat16 [4096, 8192], P('seq', 'head'), may hold values from -0.09375 to 0.09375
Outputs:
- stream: bfloat16 [8192, 4096], P(('seq', 'head'))
- next_x: bfloat16 [8192, 8192], P('seq', 'head')
The draws below stay inside these ranges and needn't reach their ends.
Inputs may be any that keep to these rules, and one draw needn't show every extreme that they name: `log_retain`: every entry is negative.
All inputs are finite; a program needn't handle non-finite values.
Results may differ from the reference program's by a relative error of at most 0.02.
Values may be sent and summed in bfloat16 or wider, within the bound.
A program may use at most 256 MiB of HBM per device.

```python
import jax
import jax.numpy as jnp
from jax import lax

D = 4096
HEADS = 128
HEAD_DIM = 64
STATE = 256
GROUPS = 8
SPAN = 256
TOK_DEV = 512
INNER = 8192
PROMPT_TOKENS = 8192
N_HEAD = 2


def draw_log_retain(key, part):
    random_key_sequence = jax.random.split(key, 7)
    fast_heads = jax.random.uniform(random_key_sequence[0], (HEADS,)) < 0.5
    fast_rate = jnp.exp(jax.random.uniform(random_key_sequence[1], (HEADS,), minval=jnp.log(0.03), maxval=jnp.log(0.1)))
    slow_rate = jax.random.uniform(random_key_sequence[2], (HEADS,), minval=0.2, maxval=0.6) / PROMPT_TOKENS
    head_decay_rate = jnp.where(fast_heads, fast_rate, slow_rate)
    token_multiplier = jnp.exp(jax.random.uniform(random_key_sequence[3], (PROMPT_TOKENS, HEADS), minval=jnp.log(0.5), maxval=jnp.log(2.0)))
    partition_factor = jnp.exp(jax.random.uniform(random_key_sequence[4], (PROMPT_TOKENS // TOK_DEV, 1, HEADS), minval=jnp.log(0.5), maxval=jnp.log(2.0)))
    partition_factor = jnp.broadcast_to(partition_factor, (PROMPT_TOKENS // TOK_DEV, TOK_DEV, HEADS)).reshape(PROMPT_TOKENS, HEADS)
    spike_selections = jax.random.randint(random_key_sequence[5], (2,), 0, PROMPT_TOKENS)
    token_positions = jnp.arange(PROMPT_TOKENS, dtype=jnp.int32)
    spike_count = jnp.sum((token_positions[:, None] == spike_selections[None, :]).astype(jnp.float32), axis=1)
    spike_loss = jax.random.uniform(random_key_sequence[6], (PROMPT_TOKENS, 1), minval=0.22, maxval=0.69)
    return -(head_decay_rate[None, :] * token_multiplier * partition_factor) - spike_count[:, None] * spike_loss


def direction_draw(key):
    return jnp.clip(jax.random.normal(jax.random.fold_in(key, 11), (D,), jnp.float32), -6.0, 6.0)


def draw_refusal(key, part):
    return direction_draw(key)


def draw_residual(key, part):
    direction = direction_draw(key)
    weight_along = 0.8 * jax.random.normal(jax.random.fold_in(key, 12), (PROMPT_TOKENS, 1), jnp.float32)
    base_values = jax.random.normal(jax.random.fold_in(key, 13), (PROMPT_TOKENS, D), jnp.float32)
    return jnp.clip(base_values + weight_along * direction[None, :], -24.0, 24.0).astype(jnp.bfloat16)


def level_of(rng, shape, shards, least, high):
    loudness, own = 1.0, jax.random.fold_in(rng, 6)
    for axis_at, shards_of in shards:
        heights = jnp.exp(jax.random.uniform(jax.random.fold_in(own, axis_at), (shards_of,), jnp.float32, least / len(shards), high / len(shards)))
        loudness = loudness * jnp.repeat(heights, shape[axis_at] // shards_of).reshape([-1 if axis == axis_at else 1 for axis in range(len(shape))])
    return loudness


def gaussian(own_key, shape, scale, reach, shards=(), kind=jnp.bfloat16):
    drawn = scale * jax.random.normal(own_key, shape, jnp.float32)
    if shards:
        drawn = drawn * level_of(own_key, shape, shards, -0.22, 0.18)
    return jnp.clip(drawn, -reach, reach).astype(kind)


def setup_inputs(seed: int = 0) -> dict:
    keys = jax.random.split(jax.random.key(seed), 13)
    xin = gaussian(keys[0], (PROMPT_TOKENS, INNER), 1.0, 6.0, ((0, 16), (1, 2)))
    gate_z = gaussian(keys[1], (PROMPT_TOKENS, INNER), 1.0, 6.0, ((0, 16), (1, 2)))
    b_proj = gaussian(keys[2], (PROMPT_TOKENS, GROUPS, STATE), (STATE ** -0.5), 0.375, ((0, 16), (1, 2)))
    c_proj = gaussian(keys[3], (PROMPT_TOKENS, GROUPS, STATE), (STATE ** -0.5), 0.375, ((0, 16), (1, 2)))
    log_retain = draw_log_retain(jax.random.fold_in(keys[12], 71), 0)
    skip_d = jnp.clip(0.5 + 1.5 * jax.random.uniform(keys[5], (HEADS,), jnp.float32) ** level_of(keys[5], (HEADS,), ((0, 2),), -0.2, 0.2), 0.5, 2.0)
    norm_gain = jnp.clip(1.0 + 0.1 * jax.random.normal(keys[6], (INNER,), jnp.float32), 0.5, 1.5)
    w_out = gaussian(keys[7], (INNER, D), INNER ** -0.5, 0.0625, ((0, 2), (1, 16)))
    residual = draw_residual(jax.random.fold_in(keys[12], 71), 0)
    refusal = draw_refusal(jax.random.fold_in(keys[12], 71), 0)
    stream_gain = jnp.clip(1.0 + 0.1 * jax.random.normal(keys[10], (D,), jnp.float32), 0.5, 1.5)
    w_in = gaussian(keys[11], (D, INNER), D ** -0.5, 0.09375, ((0, 16), (1, 2)))
    return {"xin": xin, "gate_z": gate_z, "b_proj": b_proj, "c_proj": c_proj, "log_retain": log_retain, "skip_d": skip_d, "norm_gain": norm_gain, "w_out": w_out, "residual": residual, "refusal": refusal, "stream_gain": stream_gain, "w_in": w_in}


def span_step(carry_state, inputs, skip_d, norm_gain):
    x_block, z_block, b_block, c_block, retain_block = inputs
    per_group = HEADS // GROUPS
    cum = jnp.cumsum(retain_block, axis=0)
    cum_heads = jnp.transpose(cum, (1, 0))
    scores = jnp.einsum('lgn,sgn->gls', c_block.astype(jnp.float32), b_block.astype(jnp.float32))
    scores = jnp.repeat(scores, per_group, axis=0)
    later_pos = lax.broadcasted_iota(jnp.int32, (SPAN, SPAN), 0)
    earlier_pos = lax.broadcasted_iota(jnp.int32, (SPAN, SPAN), 1)
    causal = later_pos >= earlier_pos
    gap = cum_heads[:, :, None] - cum_heads[:, None, :]
    mixing = (jnp.where(causal, jnp.exp(jnp.where(causal, gap, 0.0)), 0.0) * scores).astype(jnp.bfloat16)
    x_float = x_block.astype(jnp.float32)
    intra = jnp.einsum('hls,shp->lhp', mixing.astype(jnp.float32), x_float)
    b_heads = jnp.repeat(b_block, per_group, axis=1)
    c_heads = jnp.repeat(c_block, per_group, axis=1).astype(jnp.float32)
    carried = jnp.einsum('lhn,hnp->lhp', c_heads, carry_state, precision=lax.Precision.HIGHEST)
    carried = carried * jnp.exp(cum)[:, :, None]
    tail_decay = jnp.exp(cum_heads[:, -1:] - cum_heads)
    weighted_b = (b_heads.astype(jnp.float32) * jnp.transpose(tail_decay, (1, 0))[:, :, None]).astype(jnp.bfloat16)
    block_state = jnp.einsum('lhn,lhp->hnp', weighted_b.astype(jnp.float32), x_float)
    new_state = jnp.exp(cum_heads[:, -1])[:, None, None] * carry_state + block_state
    mixed = intra + carried + skip_d[None, :, None] * x_float
    gated = mixed * jax.nn.silu(z_block.astype(jnp.float32))
    grouped = gated.reshape(SPAN, GROUPS, per_group * HEAD_DIM)
    grouped = grouped * lax.rsqrt(lax.optimization_barrier(jnp.mean(grouped * grouped, axis=-1, keepdims=True)) + 1e-05)
    ssd_out = (grouped.reshape(SPAN, INNER) * norm_gain[None, :]).astype(jnp.bfloat16)
    return (new_state, ssd_out)

def reference(xin, gate_z, b_proj, c_proj, log_retain, skip_d, norm_gain, w_out, residual, refusal, stream_gain, w_in):
    block_total = PROMPT_TOKENS // SPAN
    x_blocks = xin.reshape(block_total, SPAN, HEADS, HEAD_DIM)
    z_blocks = gate_z.reshape(block_total, SPAN, HEADS, HEAD_DIM)
    b_blocks = b_proj.reshape(block_total, SPAN, GROUPS, STATE)
    c_blocks = c_proj.reshape(block_total, SPAN, GROUPS, STATE)
    retain_blocks = log_retain.reshape(block_total, SPAN, HEADS)
    start_state = jnp.zeros((HEADS, STATE, HEAD_DIM), jnp.float32)

    def scan_step(carry_state, inputs):
        return span_step(carry_state, inputs, skip_d, norm_gain)
    unused_state, ssd_blocks = lax.scan(scan_step, start_state, (x_blocks, z_blocks, b_blocks, c_blocks, retain_blocks))
    ssd_out = ssd_blocks.reshape(PROMPT_TOKENS, INNER)
    block_width = INNER // N_HEAD
    mixer_out = jnp.zeros((PROMPT_TOKENS, D), jnp.float32)
    for block_index in range(N_HEAD):
        lower = block_index * block_width
        partial_value = jnp.dot(ssd_out[:, lower:lower + block_width], w_out[lower:lower + block_width, :], preferred_element_type=jnp.float32).astype(jnp.bfloat16)
        mixer_out = mixer_out + partial_value.astype(jnp.float32)
    unit = refusal / jnp.sqrt(jnp.sum(refusal * refusal) + 1e-06)
    hidden = residual.astype(jnp.float32) + mixer_out
    coef = jnp.dot(hidden, unit, precision=lax.Precision.HIGHEST)
    stream = (hidden - coef[:, None] * unit[None, :]).astype(jnp.bfloat16)
    stream_float = stream.astype(jnp.float32)
    normed = (stream_float * lax.rsqrt(lax.optimization_barrier(jnp.mean(stream_float * stream_float, axis=-1, keepdims=True)) + 1e-05) * stream_gain[None, :]).astype(jnp.bfloat16)
    next_x = jnp.dot(normed, w_in, preferred_element_type=jnp.float32).astype(jnp.bfloat16)
    return (stream, next_x)
```

```python
import functools

import jax
import jax.numpy as jnp
from jax import lax
from jax.experimental import pallas as pl
from jax.experimental.pallas import tpu as pltpu
from jax.sharding import PartitionSpec as P

SPAN = 256
EXTRA = 16
VMEM_LIMIT = 48 * 1024 * 1024
IN_CHUNKS = 2


def expand(values, width):
    heads = values.shape[1]
    shape = (heads, heads * width)
    spread = lax.broadcasted_iota(jnp.int32, shape, 1) // width
    spread = (spread == lax.broadcasted_iota(jnp.int32, shape, 0)).astype(jnp.bfloat16)
    high = values.astype(jnp.bfloat16)
    low = (values - high.astype(jnp.float32)).astype(jnp.bfloat16)
    return jnp.dot(high, spread, preferred_element_type=jnp.float32) + jnp.dot(
        low, spread, preferred_element_type=jnp.float32
    )


def state_kernel(blocks, width, x_ref, b_ref, cum_ref, sent_ref, local_ref):
    state_width = b_ref.shape[1]
    slices, _, lanes = sent_ref.shape
    state = None
    total = None
    for k in range(blocks):
        rows = pl.ds(k * SPAN, SPAN)
        cum = cum_ref[0, rows, :]
        last = cum[SPAN - 1 : SPAN, :]
        scale = expand(jnp.exp(last - cum), width)
        weighted = (x_ref[rows, :].astype(jnp.float32) * scale).astype(jnp.bfloat16)
        new = lax.dot_general(
            b_ref[rows, :], weighted, (((0,), (0,)), ((), ())), preferred_element_type=jnp.float32
        )
        if state is None:
            state, total = new, last
        else:
            decay = expand(jnp.exp(jnp.broadcast_to(last, (EXTRA, last.shape[1]))), width)
            state = decay[0:1, :] * state + new
            total = total + last
        if k < blocks - 1:
            local_ref[k, :, :] = state.astype(jnp.bfloat16)
    if blocks == 1:
        local_ref[0, :, :] = jnp.zeros_like(local_ref[0])
    whole = expand(jnp.exp(jnp.broadcast_to(total, (EXTRA, total.shape[1]))), width)
    high = whole.astype(jnp.bfloat16).astype(jnp.float32)
    row = lax.broadcasted_iota(jnp.int32, whole.shape, 0)
    marks = jnp.where(row == 0, high, jnp.where(row == 1, whole - high, 0.0)).astype(jnp.bfloat16)
    state = state.astype(jnp.bfloat16)
    for i in range(slices):
        sent_ref[i, 0:state_width, :] = state[:, i * lanes : (i + 1) * lanes]
        sent_ref[i, state_width : state_width + EXTRA, :] = marks[:, i * lanes : (i + 1) * lanes]


def scan_kernel(sent_ref, out_ref):
    devices, state_width, lanes = out_ref.shape
    carry = jnp.zeros((state_width, lanes), jnp.float32)
    for k in range(devices):
        out_ref[k, :, :] = carry.astype(jnp.bfloat16)
        marks = sent_ref[k, state_width : state_width + EXTRA, :].astype(jnp.float32)
        decay = marks[0:1, :] + marks[1:2, :]
        carry = decay * carry + sent_ref[k, 0:state_width, :].astype(jnp.float32)


def output_kernel(
    blocks, width, x_ref, z_ref, b_ref, c_ref, cum_ref, cum_t_ref, skip_ref, gain_ref, in_ref,
    local_ref, out_ref,
):
    per_group = cum_ref.shape[2]
    slices = in_ref.shape[0]
    incoming = jnp.concatenate([in_ref[i] for i in range(slices)], axis=1).astype(jnp.float32)
    causal = lax.broadcasted_iota(jnp.int32, (SPAN, SPAN), 0) >= lax.broadcasted_iota(
        jnp.int32, (SPAN, SPAN), 1
    )
    first = lax.broadcasted_iota(jnp.int32, (SPAN, 2 * width), 1) < width
    before = None
    for k in range(blocks):
        rows = pl.ds(k * SPAN, SPAN)
        c_block = c_ref[rows, :]
        scores = lax.dot_general(
            c_block, b_ref[rows, :], (((1,), (1,)), ((), ())), preferred_element_type=jnp.float32
        )
        scores = jnp.where(causal, scores, 0.0)
        cum = cum_ref[0, rows, :]
        grown = expand(jnp.exp(cum), width)
        if k == 0:
            start = incoming
        else:
            decay = expand(jnp.exp(jnp.broadcast_to(before, (EXTRA, per_group))), width)
            start = decay[0:1, :] * incoming + local_ref[k - 1].astype(jnp.float32)
        last = cum[SPAN - 1 : SPAN, :]
        before = last if before is None else before + last
        carried = jnp.dot(c_block, start.astype(jnp.bfloat16), preferred_element_type=jnp.float32)
        x_block = x_ref[rows, :]
        pieces = []
        for pair in range(per_group // 2):
            x_pair = x_block[:, pair * 2 * width : (pair + 1) * 2 * width]
            both = []
            for head in (2 * pair, 2 * pair + 1):
                gap = cum[:, head : head + 1] - cum_t_ref[0, head : head + 1, rows]
                mixing = (jnp.exp(jnp.minimum(gap, 0.0)) * scores).astype(jnp.bfloat16)
                both.append(jnp.dot(mixing, x_pair, preferred_element_type=jnp.float32))
            pieces.append(jnp.where(first, both[0], both[1]))
        mixed = jnp.concatenate(pieces, axis=1) + carried * grown
        mixed = mixed + skip_ref[...] * x_block.astype(jnp.float32)
        z = z_ref[rows, :].astype(jnp.float32)
        gated = mixed * (z / (1.0 + jnp.exp(-z)))
        mean = jnp.mean(gated * gated, axis=-1, keepdims=True)
        out_ref[rows, :] = (gated * lax.rsqrt(mean + 1e-05) * gain_ref[...]).astype(jnp.bfloat16)


def mixer(xin, gate_z, b_proj, c_proj, log_retain, skip_d, norm_gain, devices):
    seq_rows, channels = xin.shape
    heads = log_retain.shape[1]
    width = channels // heads
    _, groups, state_width = b_proj.shape
    per_group = heads // groups
    group_lanes = channels // groups
    blocks = seq_rows // SPAN
    lanes = channels // devices
    slices = devices // groups
    tri = jnp.tril(jnp.ones((SPAN, SPAN), jnp.float32))
    cum = jnp.einsum(
        "ts,ksh->kth",
        tri,
        log_retain.reshape(blocks, SPAN, heads),
        precision=lax.Precision.HIGHEST,
    ).reshape(seq_rows, groups, per_group)
    cum_g = jnp.transpose(cum, (1, 0, 2))
    cum_t = jnp.transpose(cum, (1, 2, 0))
    b_flat = b_proj.reshape(seq_rows, groups * state_width)
    c_flat = c_proj.reshape(seq_rows, groups * state_width)
    params = pltpu.CompilerParams(vmem_limit_bytes=VMEM_LIMIT)
    wide = pl.BlockSpec((seq_rows, group_lanes), lambda g: (0, g))
    proj = pl.BlockSpec((seq_rows, state_width), lambda g: (0, g))
    cum_spec = pl.BlockSpec((1, seq_rows, per_group), lambda g: (g, 0, 0))
    local_count = max(blocks - 1, 1)
    local_spec = pl.BlockSpec((local_count, state_width, group_lanes), lambda g: (0, 0, g))
    sent, local = pl.pallas_call(
        functools.partial(state_kernel, blocks, width),
        grid=(groups,),
        in_specs=[wide, proj, cum_spec],
        out_specs=[
            pl.BlockSpec((slices, state_width + EXTRA, lanes), lambda g: (g, 0, 0)),
            local_spec,
        ],
        out_shape=[
            jax.ShapeDtypeStruct((devices, state_width + EXTRA, lanes), jnp.bfloat16),
            jax.ShapeDtypeStruct((local_count, state_width, channels), jnp.bfloat16),
        ],
        compiler_params=params,
        name="block_states",
    )(xin, b_flat, cum_g)
    gathered = lax.all_to_all(sent, "seq", 0, 0, tiled=True)
    starts = pl.pallas_call(
        scan_kernel,
        in_specs=[pl.BlockSpec(memory_space=pltpu.VMEM)],
        out_specs=pl.BlockSpec(memory_space=pltpu.VMEM),
        out_shape=jax.ShapeDtypeStruct((devices, state_width, lanes), jnp.bfloat16),
        compiler_params=params,
        name="state_scan",
    )(gathered)
    incoming = lax.all_to_all(starts, "seq", 0, 0, tiled=True)
    row_spec = pl.BlockSpec((1, group_lanes), lambda g: (0, g))
    return pl.pallas_call(
        functools.partial(output_kernel, blocks, width),
        grid=(groups,),
        in_specs=[
            wide,
            wide,
            proj,
            proj,
            cum_spec,
            pl.BlockSpec((1, per_group, seq_rows), lambda g: (g, 0, 0)),
            row_spec,
            row_spec,
            pl.BlockSpec((slices, state_width, lanes), lambda g: (g, 0, 0)),
            local_spec,
        ],
        out_specs=wide,
        out_shape=jax.ShapeDtypeStruct((seq_rows, channels), jnp.bfloat16),
        compiler_params=params,
        name="mixer_out",
    )(
        xin,
        gate_z,
        b_flat,
        c_flat,
        cum_g,
        cum_t,
        jnp.repeat(skip_d, width)[None, :],
        norm_gain[None, :],
        incoming,
        local,
    )


def body(
    xin,
    gate_z,
    b_proj,
    c_proj,
    log_retain,
    skip_d,
    norm_gain,
    w_out,
    residual,
    refusal,
    stream_gain,
    w_in,
):
    devices = lax.axis_size("seq")
    head_devices = lax.axis_size("head")
    place = lax.axis_index("head")
    seq_rows, channels = xin.shape
    own_rows = seq_rows // head_devices

    def shift(array, by):
        pairs = [(i, (i + by) % head_devices) for i in range(head_devices)]
        return lax.ppermute(array, "head", pairs)

    w_out_all = lax.all_gather(w_out, "seq", axis=1, tiled=True)
    in_lanes = w_in.shape[1] // IN_CHUNKS
    w_in_all = [
        lax.all_gather(w_in[:, i * in_lanes : (i + 1) * in_lanes], "seq", axis=0, tiled=True)
        for i in range(IN_CHUNKS)
    ]
    ssd_out = mixer(xin, gate_z, b_proj, c_proj, log_retain, skip_d, norm_gain, devices)

    def partial_of(index):
        rows = lax.dynamic_slice_in_dim(ssd_out, index * own_rows, own_rows, 0)
        return jnp.dot(rows, w_out_all, preferred_element_type=jnp.float32).astype(jnp.bfloat16)

    arrived = [
        shift(partial_of(lax.rem(place + by, head_devices)), by) for by in range(1, head_devices)
    ]
    mixer_out = partial_of(place).astype(jnp.float32)
    for part in arrived:
        mixer_out = mixer_out + part.astype(jnp.float32)
    unit = refusal / jnp.sqrt(jnp.sum(refusal * refusal) + 1e-06)
    hidden = residual.astype(jnp.float32) + mixer_out
    coef = jnp.sum(hidden * unit[None, :], axis=-1, keepdims=True)
    stream = (hidden - coef * unit[None, :]).astype(jnp.bfloat16)
    stream_float = stream.astype(jnp.float32)
    normed = (
        stream_float
        * lax.rsqrt(jnp.mean(stream_float * stream_float, axis=-1, keepdims=True) + 1e-05)
        * stream_gain[None, :]
    ).astype(jnp.bfloat16)
    all_rows = jnp.zeros((seq_rows, normed.shape[1]), jnp.bfloat16)
    for by in range(head_devices):
        rows = normed if by == 0 else shift(normed, by)
        source = lax.rem(place - by + head_devices, head_devices)
        all_rows = lax.dynamic_update_slice_in_dim(all_rows, rows, source * own_rows, 0)
    next_x = jnp.concatenate(
        [
            jnp.dot(all_rows, weight, preferred_element_type=jnp.float32).astype(jnp.bfloat16)
            for weight in w_in_all
        ],
        axis=1,
    )
    return (stream, next_x)


def solution(mesh):
    in_specs = (
        P("seq", "head"),
        P("seq", "head"),
        P("seq", "head", None),
        P("seq", "head", None),
        P("seq", "head"),
        P("head"),
        P("head"),
        P("head", "seq"),
        P(("seq", "head"), None),
        P(),
        P(),
        P("seq", "head"),
    )
    out_specs = (P(("seq", "head"), None), P("seq", "head"))
    return jax.shard_map(body, mesh=mesh, in_specs=in_specs, out_specs=out_specs, check_vma=False)
```

```python
import functools

import jax
import jax.numpy as jnp
from jax import lax
from jax.experimental import pallas as pl
from jax.experimental.pallas import tpu as pltpu
from jax.sharding import PartitionSpec as P

SPAN = 256
EXTRA = 16
VMEM_LIMIT = 48 * 1024 * 1024
IN_CHUNKS = 1


def expand(values, width):
    heads = values.shape[1]
    shape = (heads, heads * width)
    spread = lax.broadcasted_iota(jnp.int32, shape, 1) // width
    spread = (spread == lax.broadcasted_iota(jnp.int32, shape, 0)).astype(jnp.bfloat16)
    high = values.astype(jnp.bfloat16)
    low = (values - high.astype(jnp.float32)).astype(jnp.bfloat16)
    return jnp.dot(high, spread, preferred_element_type=jnp.float32) + jnp.dot(
        low, spread, preferred_element_type=jnp.float32
    )


def state_kernel(blocks, width, x_ref, b_ref, cum_ref, sent_ref, local_ref):
    state_width = b_ref.shape[1]
    slices, _, lanes = sent_ref.shape
    state = None
    total = None
    for k in range(blocks):
        rows = pl.ds(k * SPAN, SPAN)
        cum = cum_ref[0, rows, :]
        last = cum[SPAN - 1 : SPAN, :]
        scale = expand(jnp.exp(last - cum), width)
        weighted = (x_ref[rows, :].astype(jnp.float32) * scale).astype(jnp.bfloat16)
        new = lax.dot_general(
            b_ref[rows, :], weighted, (((0,), (0,)), ((), ())), preferred_element_type=jnp.float32
        )
        if state is None:
            state, total = new, last
        else:
            decay = expand(jnp.exp(jnp.broadcast_to(last, (EXTRA, last.shape[1]))), width)
            state = decay[0:1, :] * state + new
            total = total + last
        if k < blocks - 1:
            local_ref[k, :, :] = state.astype(jnp.bfloat16)
    if blocks == 1:
        local_ref[0, :, :] = jnp.zeros_like(local_ref[0])
    whole = expand(jnp.exp(jnp.broadcast_to(total, (EXTRA, total.shape[1]))), width)
    high = whole.astype(jnp.bfloat16).astype(jnp.float32)
    row = lax.broadcasted_iota(jnp.int32, whole.shape, 0)
    marks = jnp.where(row == 0, high, jnp.where(row == 1, whole - high, 0.0)).astype(jnp.bfloat16)
    state = state.astype(jnp.bfloat16)
    for i in range(slices):
        sent_ref[i, 0:state_width, :] = state[:, i * lanes : (i + 1) * lanes]
        sent_ref[i, state_width : state_width + EXTRA, :] = marks[:, i * lanes : (i + 1) * lanes]


def decay_of(marks):
    marks = marks.astype(jnp.float32)
    return marks[0:1, :] + marks[1:2, :]


def pair_kernel(core_ref, own_ref, other_ref, chip_ref, first_ref):
    slices, rows, lanes = own_ref.shape
    state_width = rows - EXTRA
    is_first = core_ref[0] == 0
    row = lax.broadcasted_iota(jnp.int32, (EXTRA, lanes), 0)
    for i in range(slices):
        own, other = own_ref[i], other_ref[i]
        first = jnp.where(is_first, own.astype(jnp.float32), other.astype(jnp.float32))
        second = jnp.where(is_first, other.astype(jnp.float32), own.astype(jnp.float32))
        first_ref[i, :, :] = first.astype(jnp.bfloat16)
        decay = decay_of(second[state_width:, :])
        state = decay * first[:state_width, :] + second[:state_width, :]
        chip_ref[i, 0:state_width, :] = state.astype(jnp.bfloat16)
        whole = jnp.broadcast_to(decay * decay_of(first[state_width:, :]), (EXTRA, lanes))
        high = whole.astype(jnp.bfloat16).astype(jnp.float32)
        marks = jnp.where(row == 0, high, jnp.where(row == 1, whole - high, 0.0))
        chip_ref[i, state_width:rows, :] = marks.astype(jnp.bfloat16)


def scan_kernel(sent_ref, out_ref):
    devices, state_width, lanes = out_ref.shape
    carry = jnp.zeros((state_width, lanes), jnp.float32)
    for k in range(devices):
        out_ref[k, :, :] = carry.astype(jnp.bfloat16)
        decay = decay_of(sent_ref[k, state_width : state_width + EXTRA, :])
        carry = decay * carry + sent_ref[k, 0:state_width, :].astype(jnp.float32)


def split_kernel(core_ref, start_ref, first_ref, own_ref, other_ref):
    slices, state_width, _ = start_ref.shape
    is_first = core_ref[0] == 0
    for i in range(slices):
        start = start_ref[i].astype(jnp.float32)
        decay = decay_of(first_ref[i, state_width : state_width + EXTRA, :])
        later = decay * start + first_ref[i, 0:state_width, :].astype(jnp.float32)
        own_ref[i, :, :] = jnp.where(is_first, start, later).astype(jnp.bfloat16)
        other_ref[i, :, :] = jnp.where(is_first, later, start).astype(jnp.bfloat16)


def exchange(sent, devices):
    chips = devices // 2
    _, rows, lanes = sent.shape
    state_width = rows - EXTRA
    core = lax.rem(lax.axis_index("seq"), 2)
    core_arg = jnp.reshape(core, (1,)).astype(jnp.int32)
    pairs = [(i, i + 1 - 2 * (i % 2)) for i in range(devices)]
    groups = [list(range(parity, devices, 2)) for parity in range(2)]
    params = pltpu.CompilerParams(vmem_limit_bytes=VMEM_LIMIT)
    vmem = pl.BlockSpec(memory_space=pltpu.VMEM)
    smem = pl.BlockSpec(memory_space=pltpu.SMEM)
    marked = jax.ShapeDtypeStruct((chips, rows, lanes), jnp.bfloat16)
    plain = jax.ShapeDtypeStruct((chips, state_width, lanes), jnp.bfloat16)
    own = lax.dynamic_slice_in_dim(sent, core * chips, chips, 0)
    away = lax.dynamic_slice_in_dim(sent, (1 - core) * chips, chips, 0)
    other = lax.ppermute(away, "seq", pairs)
    chip, first = pl.pallas_call(
        pair_kernel,
        in_specs=[smem, vmem, vmem],
        out_specs=[vmem, vmem],
        out_shape=[marked, marked],
        compiler_params=params,
        name="chip_states",
    )(core_arg, own, other)
    gathered = lax.all_to_all(chip, "seq", 0, 0, axis_index_groups=groups, tiled=True)
    starts = pl.pallas_call(
        scan_kernel,
        in_specs=[vmem],
        out_specs=vmem,
        out_shape=plain,
        compiler_params=params,
        name="state_scan",
    )(gathered)
    entering = lax.all_to_all(starts, "seq", 0, 0, axis_index_groups=groups, tiled=True)
    mine, theirs = pl.pallas_call(
        split_kernel,
        in_specs=[smem, vmem, vmem],
        out_specs=[vmem, vmem],
        out_shape=[plain, plain],
        compiler_params=params,
        name="core_states",
    )(core_arg, entering, first)
    received = lax.ppermute(theirs, "seq", pairs)
    both = jnp.where(core == 0, jnp.stack([mine, received]), jnp.stack([received, mine]))
    return both.reshape(devices, state_width, lanes)


def output_kernel(
    blocks, width, x_ref, z_ref, b_ref, c_ref, cum_ref, cum_t_ref, skip_ref, gain_ref, in_ref,
    local_ref, out_ref,
):
    per_group = cum_ref.shape[2]
    slices = in_ref.shape[0]
    incoming = jnp.concatenate([in_ref[i] for i in range(slices)], axis=1).astype(jnp.float32)
    causal = lax.broadcasted_iota(jnp.int32, (SPAN, SPAN), 0) >= lax.broadcasted_iota(
        jnp.int32, (SPAN, SPAN), 1
    )
    first = lax.broadcasted_iota(jnp.int32, (SPAN, 2 * width), 1) < width
    before = None
    for k in range(blocks):
        rows = pl.ds(k * SPAN, SPAN)
        c_block = c_ref[rows, :]
        scores = lax.dot_general(
            c_block, b_ref[rows, :], (((1,), (1,)), ((), ())), preferred_element_type=jnp.float32
        )
        scores = jnp.where(causal, scores, 0.0)
        cum = cum_ref[0, rows, :]
        grown = expand(jnp.exp(cum), width)
        if k == 0:
            start = incoming
        else:
            decay = expand(jnp.exp(jnp.broadcast_to(before, (EXTRA, per_group))), width)
            start = decay[0:1, :] * incoming + local_ref[k - 1].astype(jnp.float32)
        last = cum[SPAN - 1 : SPAN, :]
        before = last if before is None else before + last
        carried = jnp.dot(c_block, start.astype(jnp.bfloat16), preferred_element_type=jnp.float32)
        x_block = x_ref[rows, :]
        pieces = []
        for pair in range(per_group // 2):
            x_pair = x_block[:, pair * 2 * width : (pair + 1) * 2 * width]
            both = []
            for head in (2 * pair, 2 * pair + 1):
                gap = cum[:, head : head + 1] - cum_t_ref[0, head : head + 1, rows]
                mixing = (jnp.exp(jnp.minimum(gap, 0.0)) * scores).astype(jnp.bfloat16)
                both.append(jnp.dot(mixing, x_pair, preferred_element_type=jnp.float32))
            pieces.append(jnp.where(first, both[0], both[1]))
        mixed = jnp.concatenate(pieces, axis=1) + carried * grown
        mixed = mixed + skip_ref[...] * x_block.astype(jnp.float32)
        z = z_ref[rows, :].astype(jnp.float32)
        gated = mixed * (z / (1.0 + jnp.exp(-z)))
        mean = jnp.mean(gated * gated, axis=-1, keepdims=True)
        out_ref[rows, :] = (gated * lax.rsqrt(mean + 1e-05) * gain_ref[...]).astype(jnp.bfloat16)


def mixer(xin, gate_z, b_proj, c_proj, log_retain, skip_d, norm_gain, devices):
    seq_rows, channels = xin.shape
    heads = log_retain.shape[1]
    width = channels // heads
    _, groups, state_width = b_proj.shape
    per_group = heads // groups
    group_lanes = channels // groups
    blocks = seq_rows // SPAN
    lanes = channels // devices
    slices = devices // groups
    tri = jnp.tril(jnp.ones((SPAN, SPAN), jnp.float32))
    cum = jnp.einsum(
        "ts,ksh->kth",
        tri,
        log_retain.reshape(blocks, SPAN, heads),
        precision=lax.Precision.HIGHEST,
    ).reshape(seq_rows, groups, per_group)
    cum_g = jnp.transpose(cum, (1, 0, 2))
    cum_t = jnp.transpose(cum, (1, 2, 0))
    b_flat = b_proj.reshape(seq_rows, groups * state_width)
    c_flat = c_proj.reshape(seq_rows, groups * state_width)
    params = pltpu.CompilerParams(vmem_limit_bytes=VMEM_LIMIT)
    wide = pl.BlockSpec((seq_rows, group_lanes), lambda g: (0, g))
    proj = pl.BlockSpec((seq_rows, state_width), lambda g: (0, g))
    cum_spec = pl.BlockSpec((1, seq_rows, per_group), lambda g: (g, 0, 0))
    local_count = max(blocks - 1, 1)
    local_spec = pl.BlockSpec((local_count, state_width, group_lanes), lambda g: (0, 0, g))
    sent, local = pl.pallas_call(
        functools.partial(state_kernel, blocks, width),
        grid=(groups,),
        in_specs=[wide, proj, cum_spec],
        out_specs=[
            pl.BlockSpec((slices, state_width + EXTRA, lanes), lambda g: (g, 0, 0)),
            local_spec,
        ],
        out_shape=[
            jax.ShapeDtypeStruct((devices, state_width + EXTRA, lanes), jnp.bfloat16),
            jax.ShapeDtypeStruct((local_count, state_width, channels), jnp.bfloat16),
        ],
        compiler_params=params,
        name="block_states",
    )(xin, b_flat, cum_g)
    incoming = exchange(sent, devices)
    row_spec = pl.BlockSpec((1, group_lanes), lambda g: (0, g))
    return pl.pallas_call(
        functools.partial(output_kernel, blocks, width),
        grid=(groups,),
        in_specs=[
            wide,
            wide,
            proj,
            proj,
            cum_spec,
            pl.BlockSpec((1, per_group, seq_rows), lambda g: (g, 0, 0)),
            row_spec,
            row_spec,
            pl.BlockSpec((slices, state_width, lanes), lambda g: (g, 0, 0)),
            local_spec,
        ],
        out_specs=wide,
        out_shape=jax.ShapeDtypeStruct((seq_rows, channels), jnp.bfloat16),
        compiler_params=params,
        name="mixer_out",
    )(
        xin,
        gate_z,
        b_flat,
        c_flat,
        cum_g,
        cum_t,
        jnp.repeat(skip_d, width)[None, :],
        norm_gain[None, :],
        incoming,
        local,
    )


def body(
    xin,
    gate_z,
    b_proj,
    c_proj,
    log_retain,
    skip_d,
    norm_gain,
    w_out,
    residual,
    refusal,
    stream_gain,
    w_in,
):
    devices = lax.axis_size("seq")
    head_devices = lax.axis_size("head")
    place = lax.axis_index("head")
    seq_rows, channels = xin.shape
    own_rows = seq_rows // head_devices

    def shift(array, by):
        pairs = [(i, (i + by) % head_devices) for i in range(head_devices)]
        return lax.ppermute(array, "head", pairs)

    w_out_all = lax.all_gather(w_out, "seq", axis=1, tiled=True)
    in_lanes = w_in.shape[1] // IN_CHUNKS
    w_in_all = [
        lax.all_gather(w_in[:, i * in_lanes : (i + 1) * in_lanes], "seq", axis=0, tiled=True)
        for i in range(IN_CHUNKS)
    ]
    ssd_out = mixer(xin, gate_z, b_proj, c_proj, log_retain, skip_d, norm_gain, devices)

    def partial_of(index):
        rows = lax.dynamic_slice_in_dim(ssd_out, index * own_rows, own_rows, 0)
        return jnp.dot(rows, w_out_all, preferred_element_type=jnp.float32).astype(jnp.bfloat16)

    arrived = [
        shift(partial_of(lax.rem(place + by, head_devices)), by) for by in range(1, head_devices)
    ]
    mixer_out = partial_of(place).astype(jnp.float32)
    for part in arrived:
        mixer_out = mixer_out + part.astype(jnp.float32)
    unit = refusal / jnp.sqrt(jnp.sum(refusal * refusal) + 1e-06)
    hidden = residual.astype(jnp.float32) + mixer_out
    coef = jnp.sum(hidden * unit[None, :], axis=-1, keepdims=True)
    stream = (hidden - coef * unit[None, :]).astype(jnp.bfloat16)
    stream_float = stream.astype(jnp.float32)
    normed = (
        stream_float
        * lax.rsqrt(jnp.mean(stream_float * stream_float, axis=-1, keepdims=True) + 1e-05)
        * stream_gain[None, :]
    ).astype(jnp.bfloat16)
    all_rows = jnp.zeros((seq_rows, normed.shape[1]), jnp.bfloat16)
    for by in range(head_devices):
        rows = normed if by == 0 else shift(normed, by)
        source = lax.rem(place - by + head_devices, head_devices)
        all_rows = lax.dynamic_update_slice_in_dim(all_rows, rows, source * own_rows, 0)
    next_x = jnp.concatenate(
        [
            jnp.dot(all_rows, weight, preferred_element_type=jnp.float32).astype(jnp.bfloat16)
            for weight in w_in_all
        ],
        axis=1,
    )
    return (stream, next_x)


def solution(mesh):
    in_specs = (
        P("seq", "head"),
        P("seq", "head"),
        P("seq", "head", None),
        P("seq", "head", None),
        P("seq", "head"),
        P("head"),
        P("head"),
        P("head", "seq"),
        P(("seq", "head"), None),
        P(),
        P(),
        P("seq", "head"),
    )
    out_specs = (P(("seq", "head"), None), P("seq", "head"))
    return jax.shard_map(body, mesh=mesh, in_specs=in_specs, out_specs=out_specs, check_vma=False)
```

```python
import functools

import jax
import jax.numpy as jnp
from jax import lax
from jax.experimental import pallas as pl
from jax.experimental.pallas import tpu as pltpu
from jax.sharding import PartitionSpec as P

SPAN = 256
EXTRA = 16
VMEM_LIMIT = 48 * 1024 * 1024
TILE = 512


def expand(values, width):
    heads = values.shape[1]
    shape = (heads, heads * width)
    spread = lax.broadcasted_iota(jnp.int32, shape, 1) // width
    spread = (spread == lax.broadcasted_iota(jnp.int32, shape, 0)).astype(jnp.bfloat16)
    high = values.astype(jnp.bfloat16)
    low = (values - high.astype(jnp.float32)).astype(jnp.bfloat16)
    return jnp.dot(high, spread, preferred_element_type=jnp.float32) + jnp.dot(
        low, spread, preferred_element_type=jnp.float32
    )


def state_kernel(blocks, width, x_ref, b_ref, cum_ref, sent_ref, local_ref):
    state_width = b_ref.shape[1]
    slices, _, lanes = sent_ref.shape
    state = None
    total = None
    for k in range(blocks):
        rows = pl.ds(k * SPAN, SPAN)
        cum = cum_ref[0, rows, :]
        last = cum[SPAN - 1 : SPAN, :]
        scale = expand(jnp.exp(last - cum), width)
        weighted = (x_ref[rows, :].astype(jnp.float32) * scale).astype(jnp.bfloat16)
        new = lax.dot_general(
            b_ref[rows, :], weighted, (((0,), (0,)), ((), ())), preferred_element_type=jnp.float32
        )
        if state is None:
            state, total = new, last
        else:
            decay = expand(jnp.exp(jnp.broadcast_to(last, (EXTRA, last.shape[1]))), width)
            state = decay[0:1, :] * state + new
            total = total + last
        if k < blocks - 1:
            local_ref[k, :, :] = state.astype(jnp.bfloat16)
    if blocks == 1:
        local_ref[0, :, :] = jnp.zeros_like(local_ref[0])
    whole = expand(jnp.exp(jnp.broadcast_to(total, (EXTRA, total.shape[1]))), width)
    high = whole.astype(jnp.bfloat16).astype(jnp.float32)
    row = lax.broadcasted_iota(jnp.int32, whole.shape, 0)
    marks = jnp.where(row == 0, high, jnp.where(row == 1, whole - high, 0.0)).astype(jnp.bfloat16)
    state = state.astype(jnp.bfloat16)
    for i in range(slices):
        sent_ref[i, 0:state_width, :] = state[:, i * lanes : (i + 1) * lanes]
        sent_ref[i, state_width : state_width + EXTRA, :] = marks[:, i * lanes : (i + 1) * lanes]


def decay_of(marks):
    marks = marks.astype(jnp.float32)
    return marks[0:1, :] + marks[1:2, :]


def pair_kernel(side_ref, own_ref, other_ref, pair_ref, first_ref):
    slices, rows, lanes = own_ref.shape
    state_width = rows - EXTRA
    is_first = side_ref[0] == 0
    row = lax.broadcasted_iota(jnp.int32, (EXTRA, lanes), 0)
    for i in range(slices):
        own, other = own_ref[i], other_ref[i]
        first = jnp.where(is_first, own.astype(jnp.float32), other.astype(jnp.float32))
        second = jnp.where(is_first, other.astype(jnp.float32), own.astype(jnp.float32))
        first_ref[i, :, :] = first.astype(jnp.bfloat16)
        decay = decay_of(second[state_width:, :])
        state = decay * first[:state_width, :] + second[:state_width, :]
        pair_ref[i, 0:state_width, :] = state.astype(jnp.bfloat16)
        whole = jnp.broadcast_to(decay * decay_of(first[state_width:, :]), (EXTRA, lanes))
        high = whole.astype(jnp.bfloat16).astype(jnp.float32)
        marks = jnp.where(row == 0, high, jnp.where(row == 1, whole - high, 0.0))
        pair_ref[i, state_width:rows, :] = marks.astype(jnp.bfloat16)


def split_kernel(side_ref, start_ref, first_ref, own_ref, other_ref):
    slices, state_width, _ = start_ref.shape
    is_first = side_ref[0] == 0
    for i in range(slices):
        start = start_ref[i].astype(jnp.float32)
        decay = decay_of(first_ref[i, state_width : state_width + EXTRA, :])
        later = decay * start + first_ref[i, 0:state_width, :].astype(jnp.float32)
        own_ref[i, :, :] = jnp.where(is_first, start, later).astype(jnp.bfloat16)
        other_ref[i, :, :] = jnp.where(is_first, later, start).astype(jnp.bfloat16)


def exchange(sent, devices, reach=1):
    slices, rows, lanes = sent.shape
    half = slices // 2
    state_width = rows - EXTRA
    side = lax.rem(lax.axis_index("seq") // reach, 2)
    side_arg = jnp.reshape(side, (1,)).astype(jnp.int32)
    pairs = [(i, i ^ reach) for i in range(devices)]
    params = pltpu.CompilerParams(vmem_limit_bytes=VMEM_LIMIT)
    vmem = pl.BlockSpec(memory_space=pltpu.VMEM)
    smem = pl.BlockSpec(memory_space=pltpu.SMEM)
    marked = jax.ShapeDtypeStruct((half, rows, lanes), jnp.bfloat16)
    plain = jax.ShapeDtypeStruct((half, state_width, lanes), jnp.bfloat16)
    own = lax.dynamic_slice_in_dim(sent, side * half, half, 0)
    away = lax.dynamic_slice_in_dim(sent, (1 - side) * half, half, 0)
    other = lax.ppermute(away, "seq", pairs)
    pair, first = pl.pallas_call(
        pair_kernel,
        in_specs=[smem, vmem, vmem],
        out_specs=[vmem, vmem],
        out_shape=[marked, marked],
        compiler_params=params,
        name=f"pair_{reach}",
    )(side_arg, own, other)
    if 2 * reach < devices:
        entering = exchange(pair, devices, 2 * reach)
    else:
        entering = jnp.zeros(plain.shape, plain.dtype)
    mine, theirs = pl.pallas_call(
        split_kernel,
        in_specs=[smem, vmem, vmem],
        out_specs=[vmem, vmem],
        out_shape=[plain, plain],
        compiler_params=params,
        name=f"split_{reach}",
    )(side_arg, entering, first)
    received = lax.ppermute(theirs, "seq", pairs)
    both = jnp.where(side == 0, jnp.stack([mine, received]), jnp.stack([received, mine]))
    return both.reshape(slices, state_width, lanes)


def output_kernel(
    blocks, width, x_ref, z_ref, b_ref, c_ref, cum_ref, cum_t_ref, skip_ref, gain_ref, in_ref,
    local_ref, out_ref,
):
    per_group = cum_ref.shape[2]
    slices = in_ref.shape[0]
    incoming = jnp.concatenate([in_ref[i] for i in range(slices)], axis=1).astype(jnp.float32)
    causal = lax.broadcasted_iota(jnp.int32, (SPAN, SPAN), 0) >= lax.broadcasted_iota(
        jnp.int32, (SPAN, SPAN), 1
    )
    first = lax.broadcasted_iota(jnp.int32, (SPAN, 2 * width), 1) < width
    before = None
    for k in range(blocks):
        rows = pl.ds(k * SPAN, SPAN)
        c_block = c_ref[rows, :]
        scores = lax.dot_general(
            c_block, b_ref[rows, :], (((1,), (1,)), ((), ())), preferred_element_type=jnp.float32
        )
        scores = jnp.where(causal, scores, 0.0)
        cum = cum_ref[0, rows, :]
        grown = expand(jnp.exp(cum), width)
        if k == 0:
            start = incoming
        else:
            decay = expand(jnp.exp(jnp.broadcast_to(before, (EXTRA, per_group))), width)
            start = decay[0:1, :] * incoming + local_ref[k - 1].astype(jnp.float32)
        last = cum[SPAN - 1 : SPAN, :]
        before = last if before is None else before + last
        carried = jnp.dot(c_block, start.astype(jnp.bfloat16), preferred_element_type=jnp.float32)
        x_block = x_ref[rows, :]
        pieces = []
        for pair in range(per_group // 2):
            x_pair = x_block[:, pair * 2 * width : (pair + 1) * 2 * width]
            both = []
            for head in (2 * pair, 2 * pair + 1):
                gap = cum[:, head : head + 1] - cum_t_ref[0, head : head + 1, rows]
                mixing = (jnp.exp(jnp.minimum(gap, 0.0)) * scores).astype(jnp.bfloat16)
                both.append(jnp.dot(mixing, x_pair, preferred_element_type=jnp.float32))
            pieces.append(jnp.where(first, both[0], both[1]))
        mixed = jnp.concatenate(pieces, axis=1) + carried * grown
        mixed = mixed + skip_ref[...] * x_block.astype(jnp.float32)
        z = z_ref[rows, :].astype(jnp.float32)
        gated = mixed * (z / (1.0 + jnp.exp(-z)))
        mean = jnp.mean(gated * gated, axis=-1, keepdims=True)
        out_ref[rows, :] = (gated * lax.rsqrt(mean + 1e-05) * gain_ref[...]).astype(jnp.bfloat16)


def mixer(xin, gate_z, b_proj, c_proj, log_retain, skip_d, norm_gain, devices):
    seq_rows, channels = xin.shape
    heads = log_retain.shape[1]
    width = channels // heads
    _, groups, state_width = b_proj.shape
    per_group = heads // groups
    group_lanes = channels // groups
    blocks = seq_rows // SPAN
    lanes = channels // devices
    slices = devices // groups
    tri = jnp.tril(jnp.ones((SPAN, SPAN), jnp.float32))
    cum = jnp.einsum(
        "ts,ksh->kth",
        tri,
        log_retain.reshape(blocks, SPAN, heads),
        precision=lax.Precision.HIGHEST,
    ).reshape(seq_rows, groups, per_group)
    cum_g = jnp.transpose(cum, (1, 0, 2))
    cum_t = jnp.transpose(cum, (1, 2, 0))
    b_flat = b_proj.reshape(seq_rows, groups * state_width)
    c_flat = c_proj.reshape(seq_rows, groups * state_width)
    params = pltpu.CompilerParams(vmem_limit_bytes=VMEM_LIMIT)
    wide = pl.BlockSpec((seq_rows, group_lanes), lambda g: (0, g))
    proj = pl.BlockSpec((seq_rows, state_width), lambda g: (0, g))
    cum_spec = pl.BlockSpec((1, seq_rows, per_group), lambda g: (g, 0, 0))
    local_count = max(blocks - 1, 1)
    local_spec = pl.BlockSpec((local_count, state_width, group_lanes), lambda g: (0, 0, g))
    sent, local = pl.pallas_call(
        functools.partial(state_kernel, blocks, width),
        grid=(groups,),
        in_specs=[wide, proj, cum_spec],
        out_specs=[
            pl.BlockSpec((slices, state_width + EXTRA, lanes), lambda g: (g, 0, 0)),
            local_spec,
        ],
        out_shape=[
            jax.ShapeDtypeStruct((devices, state_width + EXTRA, lanes), jnp.bfloat16),
            jax.ShapeDtypeStruct((local_count, state_width, channels), jnp.bfloat16),
        ],
        compiler_params=params,
        name="block_states",
    )(xin, b_flat, cum_g)
    incoming = exchange(sent, devices)
    row_spec = pl.BlockSpec((1, group_lanes), lambda g: (0, g))
    return pl.pallas_call(
        functools.partial(output_kernel, blocks, width),
        grid=(groups,),
        in_specs=[
            wide,
            wide,
            proj,
            proj,
            cum_spec,
            pl.BlockSpec((1, per_group, seq_rows), lambda g: (g, 0, 0)),
            row_spec,
            row_spec,
            pl.BlockSpec((slices, state_width, lanes), lambda g: (g, 0, 0)),
            local_spec,
        ],
        out_specs=wide,
        out_shape=jax.ShapeDtypeStruct((seq_rows, channels), jnp.bfloat16),
        compiler_params=params,
        name="mixer_out",
    )(
        xin,
        gate_z,
        b_flat,
        c_flat,
        cum_g,
        cum_t,
        jnp.repeat(skip_d, width)[None, :],
        norm_gain[None, :],
        incoming,
        local,
    )


def product_kernel(rows_ref, weight_ref, out_ref):
    out_ref[...] = jnp.dot(
        rows_ref[...], weight_ref[...], preferred_element_type=jnp.float32
    ).astype(jnp.bfloat16)


def product(rows, weight):
    count, depth = rows.shape
    columns = weight.shape[1]
    tile = min(TILE, columns)
    return pl.pallas_call(
        product_kernel,
        grid=(columns // tile,),
        in_specs=[
            pl.BlockSpec((count, depth), lambda j: (0, 0)),
            pl.BlockSpec((depth, tile), lambda j: (0, j)),
        ],
        out_specs=pl.BlockSpec((count, tile), lambda j: (0, j)),
        out_shape=jax.ShapeDtypeStruct((count, columns), jnp.bfloat16),
        compiler_params=pltpu.CompilerParams(vmem_limit_bytes=VMEM_LIMIT),
        cost_estimate=pl.CostEstimate(
            flops=2 * count * depth * columns,
            bytes_accessed=2 * (count * depth + depth * columns + count * columns),
            transcendentals=0,
        ),
        name="next_x",
    )(rows, weight)


def body(
    xin,
    gate_z,
    b_proj,
    c_proj,
    log_retain,
    skip_d,
    norm_gain,
    w_out,
    residual,
    refusal,
    stream_gain,
    w_in,
):
    devices = lax.axis_size("seq")
    head_devices = lax.axis_size("head")
    place = lax.axis_index("head")
    seq_rows, channels = xin.shape
    own_rows = seq_rows // head_devices

    def shift(array, by):
        pairs = [(i, (i + by) % head_devices) for i in range(head_devices)]
        return lax.ppermute(array, "head", pairs)

    w_out_all = lax.all_gather(w_out, "seq", axis=1, tiled=True)
    w_in_all = lax.all_gather(w_in, "seq", axis=0, tiled=True)
    ssd_out = mixer(xin, gate_z, b_proj, c_proj, log_retain, skip_d, norm_gain, devices)

    def partial_of(index):
        rows = lax.dynamic_slice_in_dim(ssd_out, index * own_rows, own_rows, 0)
        return jnp.dot(rows, w_out_all, preferred_element_type=jnp.float32).astype(jnp.bfloat16)

    arrived = [
        shift(partial_of(lax.rem(place + by, head_devices)), by) for by in range(1, head_devices)
    ]
    mixer_out = partial_of(place).astype(jnp.float32)
    for part in arrived:
        mixer_out = mixer_out + part.astype(jnp.float32)
    unit = refusal / jnp.sqrt(jnp.sum(refusal * refusal) + 1e-06)
    hidden = residual.astype(jnp.float32) + mixer_out
    coef = jnp.sum(hidden * unit[None, :], axis=-1, keepdims=True)
    stream = (hidden - coef * unit[None, :]).astype(jnp.bfloat16)
    stream_float = stream.astype(jnp.float32)
    normed = (
        stream_float
        * lax.rsqrt(jnp.mean(stream_float * stream_float, axis=-1, keepdims=True) + 1e-05)
        * stream_gain[None, :]
    ).astype(jnp.bfloat16)
    all_rows = jnp.zeros((seq_rows, normed.shape[1]), jnp.bfloat16)
    for by in range(head_devices):
        rows = normed if by == 0 else shift(normed, by)
        source = lax.rem(place - by + head_devices, head_devices)
        all_rows = lax.dynamic_update_slice_in_dim(all_rows, rows, source * own_rows, 0)
    next_x = product(all_rows, w_in_all)
    return (stream, next_x)


def solution(mesh):
    in_specs = (
        P("seq", "head"),
        P("seq", "head"),
        P("seq", "head", None),
        P("seq", "head", None),
        P("seq", "head"),
        P("head"),
        P("head"),
        P("head", "seq"),
        P(("seq", "head"), None),
        P(),
        P(),
        P("seq", "head"),
    )
    out_specs = (P(("seq", "head"), None), P("seq", "head"))
    return jax.shard_map(body, mesh=mesh, in_specs=in_specs, out_specs=out_specs, check_vma=False)
```

```python
import functools

import jax
import jax.numpy as jnp
from jax import lax
from jax.experimental import pallas as pl
from jax.experimental.pallas import tpu as pltpu
from jax.sharding import PartitionSpec as P

SPAN = 256
EXTRA = 16
VMEM_LIMIT = 48 * 1024 * 1024
TILE = 512


def expand(values, width):
    heads = values.shape[1]
    shape = (heads, heads * width)
    spread = lax.broadcasted_iota(jnp.int32, shape, 1) // width
    spread = (spread == lax.broadcasted_iota(jnp.int32, shape, 0)).astype(jnp.bfloat16)
    high = values.astype(jnp.bfloat16)
    low = (values - high.astype(jnp.float32)).astype(jnp.bfloat16)
    return jnp.dot(high, spread, preferred_element_type=jnp.float32) + jnp.dot(
        low, spread, preferred_element_type=jnp.float32
    )


def state_kernel(blocks, width, x_ref, b_ref, cum_ref, sent_ref, local_ref):
    state_width = b_ref.shape[1]
    slices, _, lanes = sent_ref.shape
    state = None
    total = None
    for k in range(blocks):
        rows = pl.ds(k * SPAN, SPAN)
        cum = cum_ref[0, rows, :]
        last = cum[SPAN - 1 : SPAN, :]
        scale = expand(jnp.exp(last - cum), width)
        weighted = (x_ref[rows, :].astype(jnp.float32) * scale).astype(jnp.bfloat16)
        new = lax.dot_general(
            b_ref[rows, :], weighted, (((0,), (0,)), ((), ())), preferred_element_type=jnp.float32
        )
        if state is None:
            state, total = new, last
        else:
            decay = expand(jnp.exp(jnp.broadcast_to(last, (EXTRA, last.shape[1]))), width)
            state = decay[0:1, :] * state + new
            total = total + last
        if k < blocks - 1:
            local_ref[k, :, :] = state.astype(jnp.bfloat16)
    if blocks == 1:
        local_ref[0, :, :] = jnp.zeros_like(local_ref[0])
    whole = expand(jnp.exp(jnp.broadcast_to(total, (EXTRA, total.shape[1]))), width)
    high = whole.astype(jnp.bfloat16).astype(jnp.float32)
    row = lax.broadcasted_iota(jnp.int32, whole.shape, 0)
    marks = jnp.where(row == 0, high, jnp.where(row == 1, whole - high, 0.0)).astype(jnp.bfloat16)
    state = state.astype(jnp.bfloat16)
    for i in range(slices):
        sent_ref[i, 0:state_width, :] = state[:, i * lanes : (i + 1) * lanes]
        sent_ref[i, state_width : state_width + EXTRA, :] = marks[:, i * lanes : (i + 1) * lanes]


def decay_of(marks):
    marks = marks.astype(jnp.float32)
    return marks[0:1, :] + marks[1:2, :]


def pair_kernel(side_ref, own_ref, other_ref, pair_ref, first_ref):
    slices, rows, lanes = own_ref.shape
    state_width = rows - EXTRA
    is_first = side_ref[0] == 0
    row = lax.broadcasted_iota(jnp.int32, (EXTRA, lanes), 0)
    for i in range(slices):
        own, other = own_ref[i], other_ref[i]
        first = jnp.where(is_first, own.astype(jnp.float32), other.astype(jnp.float32))
        second = jnp.where(is_first, other.astype(jnp.float32), own.astype(jnp.float32))
        first_ref[i, :, :] = first.astype(jnp.bfloat16)
        decay = decay_of(second[state_width:, :])
        state = decay * first[:state_width, :] + second[:state_width, :]
        pair_ref[i, 0:state_width, :] = state.astype(jnp.bfloat16)
        whole = jnp.broadcast_to(decay * decay_of(first[state_width:, :]), (EXTRA, lanes))
        high = whole.astype(jnp.bfloat16).astype(jnp.float32)
        marks = jnp.where(row == 0, high, jnp.where(row == 1, whole - high, 0.0))
        pair_ref[i, state_width:rows, :] = marks.astype(jnp.bfloat16)


def split_kernel(side_ref, start_ref, first_ref, own_ref, other_ref):
    slices, state_width, _ = start_ref.shape
    is_first = side_ref[0] == 0
    for i in range(slices):
        start = start_ref[i].astype(jnp.float32)
        decay = decay_of(first_ref[i, state_width : state_width + EXTRA, :])
        later = decay * start + first_ref[i, 0:state_width, :].astype(jnp.float32)
        own_ref[i, :, :] = jnp.where(is_first, start, later).astype(jnp.bfloat16)
        other_ref[i, :, :] = jnp.where(is_first, later, start).astype(jnp.bfloat16)


def exchange(sent, devices, reach=1):
    slices, rows, lanes = sent.shape
    half = slices // 2
    state_width = rows - EXTRA
    side = lax.rem(lax.axis_index("seq") // reach, 2)
    side_arg = jnp.reshape(side, (1,)).astype(jnp.int32)
    pairs = [(i, i ^ reach) for i in range(devices)]
    params = pltpu.CompilerParams(vmem_limit_bytes=VMEM_LIMIT)
    vmem = pl.BlockSpec(memory_space=pltpu.VMEM)
    smem = pl.BlockSpec(memory_space=pltpu.SMEM)
    marked = jax.ShapeDtypeStruct((half, rows, lanes), jnp.bfloat16)
    plain = jax.ShapeDtypeStruct((half, state_width, lanes), jnp.bfloat16)
    own = lax.dynamic_slice_in_dim(sent, side * half, half, 0)
    away = lax.dynamic_slice_in_dim(sent, (1 - side) * half, half, 0)
    other = lax.ppermute(away, "seq", pairs)
    pair, first = pl.pallas_call(
        pair_kernel,
        in_specs=[smem, vmem, vmem],
        out_specs=[vmem, vmem],
        out_shape=[marked, marked],
        compiler_params=params,
        name=f"pair_{reach}",
    )(side_arg, own, other)
    if 2 * reach < devices:
        entering = exchange(pair, devices, 2 * reach)
    else:
        entering = jnp.zeros(plain.shape, plain.dtype)
    mine, theirs = pl.pallas_call(
        split_kernel,
        in_specs=[smem, vmem, vmem],
        out_specs=[vmem, vmem],
        out_shape=[plain, plain],
        compiler_params=params,
        name=f"split_{reach}",
    )(side_arg, entering, first)
    received = lax.ppermute(theirs, "seq", pairs)
    both = jnp.where(side == 0, jnp.stack([mine, received]), jnp.stack([received, mine]))
    return both.reshape(slices, state_width, lanes)


def output_kernel(
    blocks, width, x_ref, z_ref, b_ref, c_ref, cum_ref, cum_t_ref, skip_ref, gain_ref, in_ref,
    local_ref, out_ref,
):
    per_group = cum_ref.shape[2]
    slices = in_ref.shape[0]
    incoming = jnp.concatenate([in_ref[i] for i in range(slices)], axis=1).astype(jnp.float32)
    causal = lax.broadcasted_iota(jnp.int32, (SPAN, SPAN), 0) >= lax.broadcasted_iota(
        jnp.int32, (SPAN, SPAN), 1
    )
    first = lax.broadcasted_iota(jnp.int32, (SPAN, 2 * width), 1) < width
    before = None
    for k in range(blocks):
        rows = pl.ds(k * SPAN, SPAN)
        c_block = c_ref[rows, :]
        scores = lax.dot_general(
            c_block, b_ref[rows, :], (((1,), (1,)), ((), ())), preferred_element_type=jnp.float32
        )
        scores = jnp.where(causal, scores, 0.0)
        cum = cum_ref[0, rows, :]
        grown = expand(jnp.exp(cum), width)
        if k == 0:
            start = incoming
        else:
            decay = expand(jnp.exp(jnp.broadcast_to(before, (EXTRA, per_group))), width)
            start = decay[0:1, :] * incoming + local_ref[k - 1].astype(jnp.float32)
        last = cum[SPAN - 1 : SPAN, :]
        before = last if before is None else before + last
        carried = jnp.dot(c_block, start.astype(jnp.bfloat16), preferred_element_type=jnp.float32)
        x_block = x_ref[rows, :]
        pieces = []
        for pair in range(per_group // 2):
            x_pair = x_block[:, pair * 2 * width : (pair + 1) * 2 * width]
            both = []
            for head in (2 * pair, 2 * pair + 1):
                gap = cum[:, head : head + 1] - cum_t_ref[0, head : head + 1, rows]
                mixing = (jnp.exp(jnp.minimum(gap, 0.0)) * scores).astype(jnp.bfloat16)
                both.append(jnp.dot(mixing, x_pair, preferred_element_type=jnp.float32))
            pieces.append(jnp.where(first, both[0], both[1]))
        mixed = jnp.concatenate(pieces, axis=1) + carried * grown
        mixed = mixed + skip_ref[...] * x_block.astype(jnp.float32)
        z = z_ref[rows, :].astype(jnp.float32)
        gated = mixed * (z / (1.0 + jnp.exp(-z)))
        mean = jnp.mean(gated * gated, axis=-1, keepdims=True)
        out_ref[rows, :] = (gated * lax.rsqrt(mean + 1e-05) * gain_ref[...]).astype(jnp.bfloat16)


def mixer(xin, gate_z, b_proj, c_proj, log_retain, skip_d, norm_gain, devices):
    seq_rows, channels = xin.shape
    heads = log_retain.shape[1]
    width = channels // heads
    _, groups, state_width = b_proj.shape
    per_group = heads // groups
    group_lanes = channels // groups
    blocks = seq_rows // SPAN
    lanes = channels // devices
    slices = devices // groups
    tri = jnp.tril(jnp.ones((SPAN, SPAN), jnp.float32))
    cum = jnp.einsum(
        "ts,ksh->kth",
        tri,
        log_retain.reshape(blocks, SPAN, heads),
        precision=lax.Precision.HIGHEST,
    ).reshape(seq_rows, groups, per_group)
    cum_g = jnp.transpose(cum, (1, 0, 2))
    cum_t = jnp.transpose(cum, (1, 2, 0))
    b_flat = b_proj.reshape(seq_rows, groups * state_width)
    c_flat = c_proj.reshape(seq_rows, groups * state_width)
    params = pltpu.CompilerParams(vmem_limit_bytes=VMEM_LIMIT)
    wide = pl.BlockSpec((seq_rows, group_lanes), lambda g: (0, g))
    proj = pl.BlockSpec((seq_rows, state_width), lambda g: (0, g))
    cum_spec = pl.BlockSpec((1, seq_rows, per_group), lambda g: (g, 0, 0))
    local_count = max(blocks - 1, 1)
    local_spec = pl.BlockSpec((local_count, state_width, group_lanes), lambda g: (0, 0, g))
    sent, local = pl.pallas_call(
        functools.partial(state_kernel, blocks, width),
        grid=(groups,),
        in_specs=[wide, proj, cum_spec],
        out_specs=[
            pl.BlockSpec((slices, state_width + EXTRA, lanes), lambda g: (g, 0, 0)),
            local_spec,
        ],
        out_shape=[
            jax.ShapeDtypeStruct((devices, state_width + EXTRA, lanes), jnp.bfloat16),
            jax.ShapeDtypeStruct((local_count, state_width, channels), jnp.bfloat16),
        ],
        compiler_params=params,
        name="block_states",
    )(xin, b_flat, cum_g)
    incoming = exchange(sent, devices)
    row_spec = pl.BlockSpec((1, group_lanes), lambda g: (0, g))
    return pl.pallas_call(
        functools.partial(output_kernel, blocks, width),
        grid=(groups,),
        in_specs=[
            wide,
            wide,
            proj,
            proj,
            cum_spec,
            pl.BlockSpec((1, per_group, seq_rows), lambda g: (g, 0, 0)),
            row_spec,
            row_spec,
            pl.BlockSpec((slices, state_width, lanes), lambda g: (g, 0, 0)),
            local_spec,
        ],
        out_specs=wide,
        out_shape=jax.ShapeDtypeStruct((seq_rows, channels), jnp.bfloat16),
        compiler_params=params,
        name="mixer_out",
    )(
        xin,
        gate_z,
        b_flat,
        c_flat,
        cum_g,
        cum_t,
        jnp.repeat(skip_d, width)[None, :],
        norm_gain[None, :],
        incoming,
        local,
    )


def product_kernel(rows_ref, weight_ref, out_ref):
    out_ref[...] = jnp.dot(
        rows_ref[...], weight_ref[...], preferred_element_type=jnp.float32
    ).astype(jnp.bfloat16)


def product(rows, weight):
    count, depth = rows.shape
    stacked = weight.ndim == 3
    tile = weight.shape[2] if stacked else min(TILE, weight.shape[1])
    columns = weight.shape[0] * tile if stacked else weight.shape[1]
    by_shard = pl.BlockSpec((None, depth, tile), lambda j: (j, 0, 0))
    by_tile = pl.BlockSpec((depth, tile), lambda j: (0, j))
    return pl.pallas_call(
        product_kernel,
        grid=(columns // tile,),
        in_specs=[
            pl.BlockSpec((count, depth), lambda j: (0, 0)),
            by_shard if stacked else by_tile,
        ],
        out_specs=pl.BlockSpec((count, tile), lambda j: (0, j)),
        out_shape=jax.ShapeDtypeStruct((count, columns), jnp.bfloat16),
        compiler_params=pltpu.CompilerParams(vmem_limit_bytes=VMEM_LIMIT),
        cost_estimate=pl.CostEstimate(
            flops=2 * count * depth * columns,
            bytes_accessed=2 * (count * depth + depth * columns + count * columns),
            transcendentals=0,
        ),
        name="product",
    )(rows, weight)


def body(
    xin,
    gate_z,
    b_proj,
    c_proj,
    log_retain,
    skip_d,
    norm_gain,
    w_out,
    residual,
    refusal,
    stream_gain,
    w_in,
):
    devices = lax.axis_size("seq")
    head_devices = lax.axis_size("head")
    place = lax.axis_index("head")
    seq_rows, channels = xin.shape
    own_rows = seq_rows // head_devices

    def shift(array, by):
        pairs = [(i, (i + by) % head_devices) for i in range(head_devices)]
        return lax.ppermute(array, "head", pairs)

    w_out_all = lax.all_gather(w_out, "seq", axis=0)
    w_in_all = lax.all_gather(w_in, "seq", axis=0, tiled=True)
    ssd_out = mixer(xin, gate_z, b_proj, c_proj, log_retain, skip_d, norm_gain, devices)

    def partial_of(index):
        rows = lax.dynamic_slice_in_dim(ssd_out, index * own_rows, own_rows, 0)
        return product(rows, w_out_all)

    arrived = [
        shift(partial_of(lax.rem(place + by, head_devices)), by) for by in range(1, head_devices)
    ]
    mixer_out = partial_of(place).astype(jnp.float32)
    for part in arrived:
        mixer_out = mixer_out + part.astype(jnp.float32)
    unit = refusal / jnp.sqrt(jnp.sum(refusal * refusal) + 1e-06)
    hidden = residual.astype(jnp.float32) + mixer_out
    coef = jnp.sum(hidden * unit[None, :], axis=-1, keepdims=True)
    stream = (hidden - coef * unit[None, :]).astype(jnp.bfloat16)
    stream_float = stream.astype(jnp.float32)
    normed = (
        stream_float
        * lax.rsqrt(jnp.mean(stream_float * stream_float, axis=-1, keepdims=True) + 1e-05)
        * stream_gain[None, :]
    ).astype(jnp.bfloat16)
    all_rows = jnp.zeros((seq_rows, normed.shape[1]), jnp.bfloat16)
    for by in range(head_devices):
        rows = normed if by == 0 else shift(normed, by)
        source = lax.rem(place - by + head_devices, head_devices)
        all_rows = lax.dynamic_update_slice_in_dim(all_rows, rows, source * own_rows, 0)
    next_x = product(all_rows, w_in_all)
    return (stream, next_x)


def solution(mesh):
    in_specs = (
        P("seq", "head"),
        P("seq", "head"),
        P("seq", "head", None),
        P("seq", "head", None),
        P("seq", "head"),
        P("head"),
        P("head"),
        P("head", "seq"),
        P(("seq", "head"), None),
        P(),
        P(),
        P("seq", "head"),
    )
    out_specs = (P(("seq", "head"), None), P("seq", "head"))
    return jax.shard_map(body, mesh=mesh, in_specs=in_specs, out_specs=out_specs, check_vma=False)
```
